32 devices in a mesh: row: 8 (over z, y), col: 4 (over x, core).
Axes of the slice: x: 2, y: 2, z: 4, core: 2. Of those that a mesh axis runs over, the one named last changes fastest.
Arguments:
- positions: float32 [16, 3, 32768], P(None, None, 'row'), may hold values from -4 to 4
- vectors: float32 [8, 32768], P(None, 'row'), may hold values from -6 to 6
- pairs: int32 [8, 4, 10, 2], P('row', 'col'), may hold values from 0 to 15, as said below
- valid: int32 [8, 4, 10], P('row', 'col'), may hold values from 0 to 1, as said below
Outputs:
- leading: float32 [8, 32768], P(None, 'row')
The draws below stay inside these ranges and needn't reach their ends.
Inputs may be any that keep to these rules, and one draw needn't show every extreme that they name: Live slots of a cell come first and name distinct tile pairs with I <= J; no unordered pair of tiles is listed twice in the whole list; padding slots hold 0 0. a < 8, b < 16. `valid`: at most 10 live slots a cell, and some cell has all 10 live.
All inputs are finite; a program needn't handle non-finite values.
Results may differ from the reference program's by a relative error of at most 0.0003.
Values sent between devices are 32-bit elements; how exact they have to be, the bound alone decides.
A program may use at most 128 MiB of HBM per device.

```python
import jax
import jax.numpy as jnp
from jax import lax

SNAP = 16
TILE = 512
VEC = 8
MAXP = 10
GRID_ROWS = 8
GRID_COLS = 4
TRAJ = 32768
ROW_TILES = 8
SUB_TILES = 2
COL_TILES = 16


def draw_positions(key, part):
    base = jax.random.fold_in(key, 31)
    values = jax.random.uniform(base, (SNAP, 3, TRAJ), jnp.float32, -4.0, 4.0)
    return values.astype(jnp.float32)


def near_pairs(key):
    base = jax.random.fold_in(key, 77)
    key_score, key_count, key_full = jax.random.split(base, 3)
    cells = GRID_ROWS * GRID_COLS
    candidates = ROW_TILES * COL_TILES
    cell_ids = jnp.arange(cells, dtype=jnp.int32)
    grid_row = cell_ids // GRID_COLS
    grid_col = cell_ids % GRID_COLS
    codes = jnp.arange(candidates, dtype=jnp.int32)
    local_row = codes // COL_TILES
    local_col = codes % COL_TILES
    row_tile = grid_row[:, None] * ROW_TILES + local_row[None, :]
    col_tile = (local_col // SUB_TILES)[None, :] * ROW_TILES + grid_col[:, None] * SUB_TILES + (local_col % SUB_TILES)[None, :]
    allowed = row_tile <= col_tile
    full_cell = jax.random.randint(key_full, (), 0, max(cells // 2, 1))
    spread = max((1 << 29) // candidates, 2)
    score = jax.random.randint(key_score, (cells, candidates), 0, spread) * candidates + codes[None, :]
    score = score + jnp.where(allowed, 0, 1 << 30)
    forced = (cell_ids == full_cell)[:, None] & (codes == COL_TILES - 1)[None, :]
    score = jnp.where(forced, -1, score)
    order = jnp.argsort(score, axis=1, stable=True)[:, :MAXP].astype(jnp.int32)
    available = jnp.sum(allowed.astype(jnp.int32), axis=1)
    count = jax.random.randint(key_count, (cells,), max(3 * MAXP // 4, 1), MAXP + 1)
    count = jnp.where(cell_ids == full_cell, MAXP, count)
    count = jnp.minimum(count, available)
    live = jnp.arange(MAXP, dtype=jnp.int32)[None, :] < count[:, None]
    first_part = jnp.where(live, order // COL_TILES, 0)
    second_part = jnp.where(live, order % COL_TILES, 0)
    listed = jnp.stack([first_part, second_part], axis=-1).reshape(GRID_ROWS, GRID_COLS, MAXP, 2)
    return (listed.astype(jnp.int32), live.astype(jnp.int32).reshape(GRID_ROWS, GRID_COLS, MAXP))


def draw_pairs(key, part):
    return near_pairs(key)[0]


def draw_valid(key, part):
    return near_pairs(key)[1]


def levels(stream_key, extent, shards, least, top_value):
    gain, own = 1.0, jax.random.fold_in(stream_key, 6)
    for axis_at, shards_of in shards:
        steps = jnp.exp(jax.random.uniform(jax.random.fold_in(own, axis_at), (shards_of,), jnp.float32, least / len(shards), top_value / len(shards)))
        gain = gain * jnp.repeat(steps, extent[axis_at] // shards_of).reshape([-1 if axis == axis_at else 1 for axis in range(len(extent))])
    return gain


def normal_values(own_key, dims, scale, reach, cuts=(), kind=jnp.bfloat16):
    values = scale * jax.random.normal(own_key, dims, jnp.float32)
    if cuts:
        values = values * levels(own_key, dims, cuts, -0.22, 0.18)
    return jnp.clip(values, -reach, reach).astype(kind)


def setup_inputs(seed: int = 0) -> dict:
    key_list = jax.random.split(jax.random.key(seed), 5)
    return {
        "positions": draw_positions(jax.random.fold_in(key_list[4], 71), 0),
        "vectors": normal_values(key_list[1], (VEC, TRAJ), 1.0, 6.0, ((1, 8),), jnp.float32),
        "pairs": draw_pairs(jax.random.fold_in(key_list[4], 71), 0),
        "valid": draw_valid(jax.random.fold_in(key_list[4], 71), 0),
    }


def form_tile(row_part, col_part):
    total = jnp.zeros((row_part.shape[2], col_part.shape[2]), jnp.float32)
    for snapshot in range(row_part.shape[0]):
        distance = jnp.zeros_like(total)
        for component in range(3):
            spacing = row_part[snapshot, component][:, None] - col_part[snapshot, component][None, :]
            distance = distance + spacing * spacing
        total = total + jnp.exp(-0.5 * distance)
    return total

def reference(positions, vectors, pairs, valid):
    count = GRID_ROWS * GRID_COLS * MAXP
    slot_ids = jnp.arange(count, dtype=jnp.int32)
    grid_row = (slot_ids // (GRID_COLS * MAXP)).astype(jnp.int32)
    grid_col = (slot_ids // MAXP % GRID_COLS).astype(jnp.int32)
    flat_pairs = pairs.reshape(count, 2).astype(jnp.int32)
    weights = valid.reshape(count).astype(jnp.float32)

    def apply_all(field):

        def visit(total, slot):
            local_row, local_col, weight, rr, cc = slot
            row_tile = (rr * ROW_TILES + local_row).astype(jnp.int32)
            col_tile = (local_col // SUB_TILES * ROW_TILES + cc * SUB_TILES + local_col % SUB_TILES).astype(jnp.int32)
            row_start = (row_tile * TILE).astype(jnp.int32)
            col_start = (col_tile * TILE).astype(jnp.int32)
            kernel = form_tile(lax.dynamic_slice_in_dim(positions, row_start, TILE, 2), lax.dynamic_slice_in_dim(positions, col_start, TILE, 2)) * weight
            row_vec = lax.dynamic_slice_in_dim(field, row_start, TILE, 1)
            col_vec = lax.dynamic_slice_in_dim(field, col_start, TILE, 1)
            to_rows = jnp.einsum('kj,ij->ki', col_vec, kernel, precision=lax.Precision.HIGHEST)
            cross = jnp.where(row_tile != col_tile, 1.0, 0.0).astype(jnp.float32)
            to_cols = jnp.einsum('ki,ij->kj', row_vec, kernel, precision=lax.Precision.HIGHEST) * cross
            total = lax.dynamic_update_slice_in_dim(total, lax.dynamic_slice_in_dim(total, row_start, TILE, 1) + to_rows, row_start, 1)
            total = lax.dynamic_update_slice_in_dim(total, lax.dynamic_slice_in_dim(total, col_start, TILE, 1) + to_cols, col_start, 1)
            return (total, None)
        start = jnp.zeros((VEC, TRAJ), jnp.float32)
        result, _ = lax.scan(visit, start, (flat_pairs[:, 0], flat_pairs[:, 1], weights, grid_row, grid_col))
        return result
    first = apply_all(vectors)
    second = apply_all(first)
    total = lax.optimization_barrier(jnp.mean(second * second, axis=1))
    return second / jnp.sqrt(total + 1e-06)[:, None]
```

```python
import functools

import jax
import jax.numpy as jnp
from jax import lax
from jax.experimental import pallas as pl
from jax.experimental.pallas import tpu as pltpu
from jax.sharding import PartitionSpec as P

TILE = 512
GROUP = 8
MESH = pl.DeviceIdType.MESH


def pieces(x):
    high = x.astype(jnp.bfloat16).astype(jnp.float32)
    rest = x - high
    mid = rest.astype(jnp.bfloat16).astype(jnp.float32)
    return high, mid, rest - mid


def stacked(v):
    high = v.astype(jnp.bfloat16).astype(jnp.float32)
    return jnp.concatenate([high, v - high], axis=0).astype(jnp.bfloat16)


def features(x):
    x1, x2, x3 = pieces(x)
    sq = x * x
    norm = -0.5 * (sq[:GROUP] + sq[GROUP : 2 * GROUP] + sq[2 * GROUP :])
    return (x1, x2, x3), jnp.concatenate(pieces(norm), axis=0)


def kernel(
    n_row, n_col, nz, ny, info_ref, x_ref, out_ref, tot_ref,
    far_first, far_last, partial_k, k_high, k_low, to_row, to_col,
    row_sum, col_sum, row_recv, col_recv, own_buf,
    first_row, first_col, second_row, sq_recv, tot_recv,
    ssem, rsem, local_sem,
):
    slots = to_row.shape[0]
    row_tiles = x_ref.shape[0]
    far = (far_first, far_last)
    col_tiles = far_first.shape[0]
    share = col_tiles // n_row
    chunks = len(far)
    depth = 3 * GROUP
    vec_at = chunks * depth
    r = lax.axis_index("row")
    c = lax.axis_index("col")
    z, y = r // ny, r % ny

    barrier = pltpu.get_barrier_semaphore()
    for k in range(1, n_row):
        pl.semaphore_signal(barrier, inc=1, device_id={"row": (r + k) % n_row}, device_id_type=MESH)
    for k in range(1, n_col):
        pl.semaphore_signal(barrier, inc=1, device_id={"col": (c + k) % n_col}, device_id_type=MESH)
    pl.semaphore_wait(barrier, n_row + n_col - 2)

    sends = []
    counter = [0]

    def next_sem():
        counter[0] += 1
        return counter[0] - 1

    def copy(src, dst, at, device):
        return pltpu.make_async_remote_copy(
            src_ref=src, dst_ref=dst, send_sem=ssem.at[at], recv_sem=rsem.at[at],
            device_id=device, device_id_type=MESH,
        )

    def rows_of(chunk):
        if chunk == chunks - 1:
            return pl.ds(chunk * depth, depth + 8)
        return pl.ds(chunk * depth, depth)

    def place(row, chunk):
        return far[chunk].at[pl.ds(row * share, share)]

    def own(chunk):
        return x_ref.at[pl.ds(c * share, share), rows_of(chunk)]

    z_sem = [[next_sem() for _ in range(nz)] for _ in range(chunks)]
    y_sem = [[[next_sem() for _ in range(ny)] for _ in range(nz)] for _ in range(chunks)]

    def z_copy(chunk, k):
        return copy(own(chunk), place(r, chunk), z_sem[chunk][k], {"row": (z + k) % nz * ny + y})

    def z_arrival(chunk, k):
        row = (z - k + nz) % nz * ny + y
        return copy(own(chunk), place(row, chunk), z_sem[chunk][k], {"row": (z + k) % nz * ny + y})

    def y_copy(chunk, k, j):
        row = (z - k + nz) % nz * ny + y
        src = own(chunk) if k == 0 else place(row, chunk)
        return copy(src, place(row, chunk), y_sem[chunk][k][j], {"row": z * ny + (y + j) % ny})

    def y_arrival(chunk, k, j):
        row = (z - k + nz) % nz * ny + (y - j + ny) % ny
        return copy(own(chunk), place(row, chunk), y_sem[chunk][k][j], {"row": z * ny + (y + j) % ny})

    def start_z(chunk):
        for k in reversed(range(1, nz)):
            z_copy(chunk, k).start()
        for j in range(1, ny):
            y_copy(chunk, 0, j).start()

    def forward(chunk, k):
        z_arrival(chunk, k).wait_recv()
        for j in range(1, ny):
            y_copy(chunk, k, j).start()

    def await_y(chunk):
        for k in range(nz):
            for j in range(1, ny):
                y_arrival(chunk, k, j).wait_recv()

    start_z(0)
    for chunk in range(chunks):
        mine = pltpu.make_async_copy(own(chunk), place(r, chunk), local_sem.at[chunk])
        mine.start()
        mine.wait()
    for k in range(1, nz):
        forward(0, k)
    start_z(1)
    await_y(0)

    def apply_slot(slot, near_row, near_col):
        high, low = k_high[slot], k_low[slot]
        vr, vc = stacked(near_row), stacked(near_col)
        nt = (((1,), (1,)), ((), ()))
        nn = (((1,), (0,)), ((), ()))
        dot = functools.partial(lax.dot_general, preferred_element_type=jnp.float32)
        rows = dot(vc, high, nt) + dot(vc, low, nt)
        cols = dot(vr, high, nn) + dot(vr, low, nn)
        to_row[slot] = rows[:8] + rows[8:]
        to_col[slot] = cols[:8] + cols[8:]

    def form(slot, chunk):
        a, b = info_ref[2 * slot], info_ref[2 * slot + 1]
        (x1, x2, x3), nx = features(x_ref[a, chunk * depth : (chunk + 1) * depth])
        (y1, y2, y3), ny_ = features(far[chunk][b, :depth])
        one = jnp.ones((depth, TILE), jnp.float32)
        left = jnp.concatenate([x1, x1, x2, x1, x2, x3, nx, one], axis=0)
        left = jnp.transpose(left).astype(jnp.bfloat16)
        right = jnp.concatenate([y1, y2, y1, y3, y2, y1, one, ny_], axis=0).astype(jnp.bfloat16)
        right = right.reshape(8 * depth // 16, 16, TILE)
        spot = lax.broadcasted_iota(jnp.int32, (16, TILE), 0) % GROUP
        total = None
        for s in range(GROUP):
            keep = jnp.where(spot == s, 1.0, 0.0).astype(jnp.bfloat16)
            part = (right * keep[None]).reshape(8 * depth, TILE)
            term = jnp.exp(jnp.dot(left, part, preferred_element_type=jnp.float32))
            total = term if total is None else total + term
        return total, a, b

    for chunk in range(chunks):
        last = chunk == chunks - 1

        def body(slot, carry, chunk=chunk, last=last):
            total, a, b = form(slot, chunk)
            if chunk > 0:
                total = total + partial_k[slot]
            if not last:
                partial_k[slot] = total
                for k in range(1, nz):
                    at = min(slots - 1, k * slots // nz)

                    @pl.when(slot == at)
                    def _():
                        forward(chunk + 1, k)
            else:
                high = total.astype(jnp.bfloat16)
                k_high[slot] = high
                k_low[slot] = (total - high.astype(jnp.float32)).astype(jnp.bfloat16)
                apply_slot(
                    slot, x_ref[a, vec_at : vec_at + 8], far[chunk][b, depth:]
                )
            return carry

        lax.fori_loop(0, slots, body, 0)
        if not last:
            await_y(chunk + 1)

    def exchange(p):
        arrivals = []
        for t in range(col_tiles):
            acc = jnp.zeros((8, TILE), jnp.float32)
            for slot in range(slots):
                a, b = info_ref[2 * slot], info_ref[2 * slot + 1]
                cross = r * row_tiles + a != b // share * row_tiles + c * share + b % share
                live = info_ref[2 * slots + slot]
                weight = jnp.where((b == t) & cross, live, 0).astype(jnp.float32)
                acc = acc + weight * to_col[slot]
            col_sum[p, t] = acc
        for k in range(1, n_row):
            to = (r + k) % n_row
            one = copy(
                col_sum.at[p, pl.ds(to * share, share)], col_recv.at[p, k], next_sem(), {"row": to}
            )
            one.start()
            arrivals.append(one)
        for t in range(row_tiles):
            acc = jnp.zeros((8, TILE), jnp.float32)
            for slot in range(slots):
                live = info_ref[2 * slots + slot]
                weight = jnp.where(info_ref[2 * slot] == t, live, 0).astype(jnp.float32)
                acc = acc + weight * to_row[slot]
            row_sum[p, t] = acc
        for k in range(1, n_col):
            to = (c + k) % n_col
            one = copy(
                row_sum.at[p, pl.ds(to * share, share)], row_recv.at[p, k], next_sem(), {"col": to}
            )
            one.start()
            arrivals.append(one)
        sends.extend(arrivals)
        total = row_sum[p, pl.ds(c * share, share)] + col_sum[p, pl.ds(r * share, share)]
        for one in arrivals:
            one.wait_recv()
        for k in range(1, n_col):
            total = total + row_recv[p, k]
        for k in range(1, n_row):
            total = total + col_recv[p, k]
        own_buf[p] = total
        return total

    def spread(src, dst_of, axis):
        size, me = (n_row, r) if axis == "row" else (n_col, c)
        arrivals = []
        for k in range(1, size):
            at = next_sem()
            one = copy(src, dst_of(me), at, {axis: (me + k) % size})
            one.start()
            sends.append(one)
            arrivals.append(copy(src, dst_of((me - k + size) % size), at, {axis: (me + k) % size}))
        return arrivals

    total = exchange(0)
    arrivals = spread(own_buf.at[0], lambda i: first_col.at[pl.ds(i * share, share)], "row")
    arrivals += spread(own_buf.at[0], lambda i: first_row.at[pl.ds(i * share, share)], "col")
    first_col[pl.ds(r * share, share)] = total
    first_row[pl.ds(c * share, share)] = total
    for one in arrivals:
        one.wait_recv()

    def again(slot, carry):
        apply_slot(slot, first_row[info_ref[2 * slot]], first_col[info_ref[2 * slot + 1]])
        return carry

    lax.fori_loop(0, slots, again, 0)

    total = exchange(1)
    squares = jnp.sum(jnp.sum(total * total, axis=0), axis=1, keepdims=True)
    sq_recv[r] = jnp.broadcast_to(squares, (8, 128))
    square_arrivals = spread(sq_recv.at[r], lambda i: sq_recv.at[i], "row")
    arrivals = spread(own_buf.at[1], lambda i: second_row.at[pl.ds(i * share, share)], "col")
    second_row[pl.ds(c * share, share)] = total
    for one in square_arrivals:
        one.wait_recv()
    tot_recv[c] = jnp.sum(sq_recv[...], axis=0)
    total_arrivals = spread(tot_recv.at[c], lambda i: tot_recv.at[i], "col")
    for one in arrivals:
        one.wait_recv()
    for t in range(row_tiles):
        out_ref[:, t * TILE : (t + 1) * TILE] = second_row[t]
    for one in total_arrivals:
        one.wait_recv()
    tot_ref[...] = jnp.sum(tot_recv[...], axis=0)

    for chunk in range(chunks):
        for k in range(1, nz):
            z_copy(chunk, k).wait_send()
        for k in range(nz):
            for j in range(1, ny):
                y_copy(chunk, k, j).wait_send()
    for one in sends:
        one.wait_send()


def per_device(n_row, n_col, positions, vectors, pairs, valid):
    snaps, _, block = positions.shape
    row_tiles = block // TILE
    share = row_tiles // n_col
    col_tiles = share * n_row
    slots = pairs.shape[2]
    vec = vectors.shape[0]
    ny = 1
    while ny * ny * 4 <= n_row:
        ny *= 2
    nz = n_row // ny
    chunks = snaps // GROUP
    spread = positions.reshape(chunks, GROUP, 3, block).transpose(0, 2, 1, 3)
    both = jnp.concatenate([spread.reshape(3 * snaps, block), vectors], axis=0)
    depth = both.shape[0]
    tiled = both.reshape(depth, row_tiles, TILE).transpose(1, 0, 2)
    info = jnp.concatenate([pairs.reshape(2 * slots), valid.reshape(slots)])
    copies = chunks * (nz + nz * ny) + 3 * (n_row + n_col) + n_row + 2 * n_col
    f32 = jnp.float32
    vm = pltpu.VMEM
    second, total = pl.pallas_call(
        functools.partial(kernel, n_row, n_col, nz, ny),
        out_shape=(
            jax.ShapeDtypeStruct((vec, block), f32),
            jax.ShapeDtypeStruct((vec, 128), f32),
        ),
        in_specs=[
            pl.BlockSpec(memory_space=pltpu.SMEM),
            pl.BlockSpec(memory_space=pltpu.VMEM),
        ],
        out_specs=[pl.BlockSpec(memory_space=pltpu.VMEM)] * 2,
        scratch_shapes=[
            vm((col_tiles, 3 * GROUP, TILE), f32),
            vm((col_tiles, 3 * GROUP + vec, TILE), f32),
            vm((slots, TILE, TILE), f32),
            vm((slots, TILE, TILE), jnp.bfloat16),
            vm((slots, TILE, TILE), jnp.bfloat16),
            vm((slots, vec, TILE), f32),
            vm((slots, vec, TILE), f32),
            vm((2, row_tiles, vec, TILE), f32),
            vm((2, col_tiles, vec, TILE), f32),
            vm((2, n_col, share, vec, TILE), f32),
            vm((2, n_row, share, vec, TILE), f32),
            vm((2, share, vec, TILE), f32),
            vm((row_tiles, vec, TILE), f32),
            vm((col_tiles, vec, TILE), f32),
            vm((row_tiles, vec, TILE), f32),
            vm((n_row, vec, 128), f32),
            vm((n_col, vec, 128), f32),
            pltpu.SemaphoreType.DMA((copies,)),
            pltpu.SemaphoreType.DMA((copies,)),
            pltpu.SemaphoreType.DMA((chunks,)),
        ],
        compiler_params=pltpu.CompilerParams(
            collective_id=0, has_side_effects=True, vmem_limit_bytes=52 * 2**20
        ),
    )(info, tiled)
    mean = total[:, :1] / (block * n_row)
    return second / jnp.sqrt(mean + 1e-06)


def solution(mesh):
    placed = (
        P(None, None, "row"),
        P(None, "row"),
        P("row", "col", None, None),
        P("row", "col", None),
    )
    body = functools.partial(per_device, mesh.shape["row"], mesh.shape["col"])
    return jax.shard_map(body, mesh=mesh, in_specs=placed, out_specs=P(None, "row"), check_vma=False)
```

```python
import functools

import jax
import jax.numpy as jnp
from jax import lax
from jax.experimental import pallas as pl
from jax.experimental.pallas import tpu as pltpu
from jax.sharding import PartitionSpec as P

TILE = 512
GROUP = 8
MESH = pl.DeviceIdType.MESH


def pieces(x):
    high = x.astype(jnp.bfloat16).astype(jnp.float32)
    rest = x - high
    mid = rest.astype(jnp.bfloat16).astype(jnp.float32)
    return high, mid, rest - mid


def stacked(v):
    high = v.astype(jnp.bfloat16).astype(jnp.float32)
    return jnp.concatenate([high, v - high], axis=0).astype(jnp.bfloat16)


def features(x):
    x1, x2, x3 = pieces(x)
    sq = x * x
    norm = -0.5 * (sq[:GROUP] + sq[GROUP : 2 * GROUP] + sq[2 * GROUP :])
    return x1, x2, x3, jnp.concatenate(pieces(norm), axis=0)


def halves(rows):
    parts = [rows[i * GROUP : (i + 1) * GROUP] for i in range(24)]
    half = GROUP // 2
    first = lax.broadcasted_iota(jnp.int32, (GROUP, TILE), 0) < half
    turned = [jnp.concatenate([part[half:], part[:half]], axis=0) for part in parts]
    fill = jnp.zeros((4 * GROUP, TILE), jnp.float32)
    early = [jnp.where(first, parts[i], turned[i + 1]) for i in range(0, 24, 2)]
    late = [jnp.where(first, turned[i], parts[i + 1]) for i in range(0, 24, 2)]
    return jnp.concatenate(early + [fill], axis=0), jnp.concatenate(late + [fill], axis=0)


def kernel(
    n_row, n_col, nz, ny, pairs_ref, valid_ref, pos_ref, vec_ref, out_ref, tot_ref,
    far_early, far_late, far_vec, row_vec, left_ref, partial_k, k_high, k_low, to_row, to_col,
    row_sum, col_sum, row_recv, col_recv, own_buf,
    first_row, first_col, second_row, sq_recv, tot_recv,
    weight_ref, ssem, rsem, local_sem,
):
    slots = to_row.shape[0]
    row_tiles = pos_ref.shape[2] // TILE
    share = row_tiles // n_col
    col_tiles = share * n_row
    far = (far_early, far_late, far_vec)
    chunks = 2
    depth = 3 * GROUP
    r = lax.axis_index("row")
    c = lax.axis_index("col")
    z, y = r // ny, r % ny

    def tile_at(tile):
        return pl.ds(pl.multiple_of(tile * TILE, TILE), TILE)

    locals_ = []
    for chunk in range(chunks + 1):
        for t in range(share):
            cut = tile_at(c * share + t)
            src = vec_ref.at[:, cut]
            if chunk < chunks:
                src = pos_ref.at[:, pl.ds(chunk * GROUP, GROUP), cut]
            mine = pltpu.make_async_copy(
                src, far[chunk].at[r * share + t], local_sem.at[chunk * share + t]
            )
            mine.start()
            locals_.append(mine)
    for t in range(row_tiles):
        row_vec[t] = vec_ref[:, t * TILE : (t + 1) * TILE]

    barrier = pltpu.get_barrier_semaphore()
    for k in range(1, n_row):
        pl.semaphore_signal(barrier, inc=1, device_id={"row": (r + k) % n_row}, device_id_type=MESH)
    for k in range(1, n_col):
        pl.semaphore_signal(barrier, inc=1, device_id={"col": (c + k) % n_col}, device_id_type=MESH)
    pl.semaphore_wait(barrier, n_row + n_col - 2)

    sends = []
    counter = [0]

    def next_sem():
        counter[0] += 1
        return counter[0] - 1

    def copy(src, dst, at, device):
        return pltpu.make_async_remote_copy(
            src_ref=src, dst_ref=dst, send_sem=ssem.at[at], recv_sem=rsem.at[at],
            device_id=device, device_id_type=MESH,
        )

    def place(row, chunk):
        return far[chunk].at[pl.ds(row * share, share)]

    def own(chunk):
        return place(r, chunk)

    z_sem = [[next_sem() for _ in range(nz)] for _ in range(chunks + 1)]
    y_sem = [[[next_sem() for _ in range(ny)] for _ in range(nz)] for _ in range(chunks + 1)]

    def z_copy(chunk, k):
        return copy(own(chunk), place(r, chunk), z_sem[chunk][k], {"row": (z + k) % nz * ny + y})

    def z_arrival(chunk, k):
        row = (z - k + nz) % nz * ny + y
        return copy(own(chunk), place(row, chunk), z_sem[chunk][k], {"row": (z + k) % nz * ny + y})

    def y_copy(chunk, k, j):
        row = (z - k + nz) % nz * ny + y
        src = own(chunk) if k == 0 else place(row, chunk)
        return copy(src, place(row, chunk), y_sem[chunk][k][j], {"row": z * ny + (y + j) % ny})

    def y_arrival(chunk, k, j):
        row = (z - k + nz) % nz * ny + (y - j + ny) % ny
        return copy(own(chunk), place(row, chunk), y_sem[chunk][k][j], {"row": z * ny + (y + j) % ny})

    def start_z(chunk):
        for k in reversed(range(1, nz)):
            z_copy(chunk, k).start()
        for j in range(1, ny):
            y_copy(chunk, 0, j).start()

    def forward(chunk, k):
        z_arrival(chunk, k).wait_recv()
        for j in range(1, ny):
            y_copy(chunk, k, j).start()

    def await_y(chunk):
        for k in range(nz):
            for j in range(1, ny):
                y_arrival(chunk, k, j).wait_recv()

    for mine in locals_:
        mine.wait()
    start_z(0)
    one = jnp.ones((depth, TILE), jnp.float32)

    def prepare(tile, carry):
        for chunk in range(chunks):
            x1, x2, x3, nx = features(
                pos_ref[:, chunk * GROUP : (chunk + 1) * GROUP, tile_at(tile)].reshape(depth, TILE)
            )
            rows = jnp.concatenate([x1, x1, x2, x1, x2, x3, nx, one], axis=0)
            for g, part in enumerate(halves(rows)):
                left_ref[tile, 2 * chunk + g] = jnp.transpose(part).astype(jnp.bfloat16)
        for k in range(1, nz):

            @pl.when(tile == k * row_tiles // nz)
            def _():
                forward(0, k)

        return carry

    lax.fori_loop(0, row_tiles, prepare, 0)
    for slot in range(slots):
        a, b, live = pairs_ref[0, 0, 0, slot], pairs_ref[0, 0, 1, slot], valid_ref[0, 0, slot]
        cross = r * row_tiles + a != b // share * row_tiles + c * share + b % share
        both = jnp.where(cross, live, 0)
        for t in range(row_tiles):
            weight_ref[t * slots + slot] = jnp.where(a == t, live, 0).astype(jnp.float32)
        for t in range(col_tiles):
            weight_ref[(row_tiles + t) * slots + slot] = jnp.where(b == t, both, 0).astype(jnp.float32)
    start_z(1)
    start_z(2)
    await_y(0)

    def apply_slot(slot, near_row, near_col):
        high, low = k_high[slot], k_low[slot]
        vr, vc = stacked(near_row), stacked(near_col)
        nt = (((1,), (1,)), ((), ()))
        nn = (((1,), (0,)), ((), ()))
        dot = functools.partial(lax.dot_general, preferred_element_type=jnp.float32)
        rows = dot(vc, high, nt) + dot(vc, low, nt)
        cols = dot(vr, high, nn) + dot(vr, low, nn)
        to_row[slot] = rows[:8] + rows[8:]
        to_col[slot] = cols[:8] + cols[8:]

    def apply_first(slot):
        a, b = pairs_ref[0, 0, 0, slot], pairs_ref[0, 0, 1, slot]
        apply_slot(slot, row_vec[a], far_vec[b])

    def form(slot, chunk):
        a, b = pairs_ref[0, 0, 0, slot], pairs_ref[0, 0, 1, slot]
        y1, y2, y3, ny_ = features(
            far[chunk][b].reshape(depth, TILE)
        )
        rows = jnp.concatenate([y1, y2, y1, y3, y2, y1, one, ny_], axis=0)
        spot = lax.broadcasted_iota(jnp.int32, (16, TILE), 0) % 4
        masked = []
        for part in halves(rows):
            part = part.astype(jnp.bfloat16).reshape(8, 16, TILE)
            for s in range(4):
                keep = jnp.where(spot == s, 1.0, 0.0).astype(jnp.bfloat16)
                masked.append((part * keep[None]).reshape(128, TILE))
        for at in range(0, TILE, 128):
            cut = slice(at, at + 128)
            total = None
            for pair in range(4):
                two = jnp.concatenate([masked[2 * pair][:, cut], masked[2 * pair + 1][:, cut]], axis=1)
                left = left_ref[a, 2 * chunk + pair // 2]
                term = jnp.exp(jnp.dot(left, two, preferred_element_type=jnp.float32))
                term = term[:, :128] + term[:, 128:]
                total = term if total is None else total + term
            if chunk > 0:
                total = total + partial_k[slot, :, cut]
            if chunk < chunks - 1:
                partial_k[slot, :, cut] = total
            else:
                high = total.astype(jnp.bfloat16)
                k_high[slot, :, cut] = high
                k_low[slot, :, cut] = (total - high.astype(jnp.float32)).astype(jnp.bfloat16)

    for chunk in range(chunks):
        last = chunk == chunks - 1

        def body(slot, carry, chunk=chunk, last=last):
            if last:
                apply_first(jnp.maximum(slot - 1, 0))
            form(slot, chunk)
            if not last:
                for k in range(1, nz):

                    @pl.when(slot == min(slots - 1, k * slots // nz))
                    def _():
                        forward(chunk + 1, k)
                        forward(chunk + 2, k)

            return carry

        if last:
            form(0, chunk)
            lax.fori_loop(1, slots, body, 0)
            apply_first(slots - 1)
        else:
            lax.fori_loop(0, slots, body, 0)
            await_y(chunk + 1)
            await_y(chunk + 2)

    def exchange(p):
        arrivals = []
        for t in range(col_tiles):
            acc = jnp.zeros((8, TILE), jnp.float32)
            for slot in range(slots):
                acc = acc + weight_ref[(row_tiles + t) * slots + slot] * to_col[slot]
            col_sum[p, t] = acc
        for k in range(1, n_row):
            to = (r + k) % n_row
            one = copy(
                col_sum.at[p, pl.ds(to * share, share)], col_recv.at[p, k], next_sem(), {"row": to}
            )
            one.start()
            arrivals.append(one)
        for t in range(row_tiles):
            acc = jnp.zeros((8, TILE), jnp.float32)
            for slot in range(slots):
                acc = acc + weight_ref[t * slots + slot] * to_row[slot]
            row_sum[p, t] = acc
        for k in range(1, n_col):
            to = (c + k) % n_col
            one = copy(
                row_sum.at[p, pl.ds(to * share, share)], row_recv.at[p, k], next_sem(), {"col": to}
            )
            one.start()
            arrivals.append(one)
        sends.extend(arrivals)
        total = row_sum[p, pl.ds(c * share, share)] + col_sum[p, pl.ds(r * share, share)]
        for one in arrivals:
            one.wait_recv()
        for k in range(1, n_col):
            total = total + row_recv[p, k]
        for k in range(1, n_row):
            total = total + col_recv[p, k]
        own_buf[p] = total
        return total

    def spread(src, dst_of, axis):
        size, me = (n_row, r) if axis == "row" else (n_col, c)
        arrivals = []
        for k in range(1, size):
            at = next_sem()
            one = copy(src, dst_of(me), at, {axis: (me + k) % size})
            one.start()
            sends.append(one)
            arrivals.append(copy(src, dst_of((me - k + size) % size), at, {axis: (me + k) % size}))
        return arrivals

    total = exchange(0)
    arrivals = spread(own_buf.at[0], lambda i: first_col.at[pl.ds(i * share, share)], "row")
    arrivals += spread(own_buf.at[0], lambda i: first_row.at[pl.ds(i * share, share)], "col")
    first_col[pl.ds(r * share, share)] = total
    first_row[pl.ds(c * share, share)] = total
    for one in arrivals:
        one.wait_recv()

    def again(slot, carry):
        a, b = pairs_ref[0, 0, 0, slot], pairs_ref[0, 0, 1, slot]
        apply_slot(slot, first_row[a], first_col[b])
        return carry

    lax.fori_loop(0, slots, again, 0)

    total = exchange(1)
    squares = jnp.sum(jnp.sum(total * total, axis=0), axis=1, keepdims=True)
    sq_recv[r] = jnp.broadcast_to(squares, (8, 128))
    square_arrivals = spread(sq_recv.at[r], lambda i: sq_recv.at[i], "row")
    arrivals = spread(own_buf.at[1], lambda i: second_row.at[pl.ds(i * share, share)], "col")
    second_row[pl.ds(c * share, share)] = total
    for one in square_arrivals:
        one.wait_recv()
    tot_recv[c] = jnp.sum(sq_recv[...], axis=0)
    total_arrivals = spread(tot_recv.at[c], lambda i: tot_recv.at[i], "col")
    for one in arrivals:
        one.wait_recv()
    for t in range(row_tiles):
        out_ref[:, t * TILE : (t + 1) * TILE] = second_row[t]
    for one in total_arrivals:
        one.wait_recv()
    tot_ref[...] = jnp.sum(tot_recv[...], axis=0)

    for chunk in range(chunks + 1):
        for k in range(1, nz):
            z_copy(chunk, k).wait_send()
        for k in range(nz):
            for j in range(1, ny):
                y_copy(chunk, k, j).wait_send()
    for one in sends:
        one.wait_send()


def per_device(n_row, n_col, positions, vectors, pairs, valid):
    snaps, _, block = positions.shape
    row_tiles = block // TILE
    share = row_tiles // n_col
    col_tiles = share * n_row
    slots = pairs.shape[2]
    vec = vectors.shape[0]
    ny = 1
    while ny * ny * 4 <= n_row:
        ny *= 2
    nz = n_row // ny
    chunks = snaps // GROUP
    copies = (chunks + 1) * (nz + nz * ny) + 3 * (n_row + n_col) + n_row + 2 * n_col
    f32 = jnp.float32
    vm = pltpu.VMEM
    second, total = pl.pallas_call(
        functools.partial(kernel, n_row, n_col, nz, ny),
        out_shape=(
            jax.ShapeDtypeStruct((vec, block), f32),
            jax.ShapeDtypeStruct((vec, 128), f32),
        ),
        in_specs=[
            pl.BlockSpec(memory_space=pltpu.SMEM),
            pl.BlockSpec(memory_space=pltpu.SMEM),
            pl.BlockSpec(memory_space=pltpu.VMEM),
            pl.BlockSpec(memory_space=pltpu.VMEM),
        ],
        out_specs=[pl.BlockSpec(memory_space=pltpu.VMEM)] * 2,
        scratch_shapes=[
            vm((col_tiles, 3, GROUP, TILE), f32),
            vm((col_tiles, 3, GROUP, TILE), f32),
            vm((col_tiles, vec, TILE), f32),
            vm((row_tiles, vec, TILE), f32),
            vm((row_tiles, 2 * chunks, TILE, 128), jnp.bfloat16),
            vm((slots, TILE, TILE), f32),
            vm((slots, TILE, TILE), jnp.bfloat16),
            vm((slots, TILE, TILE), jnp.bfloat16),
            vm((slots, vec, TILE), f32),
            vm((slots, vec, TILE), f32),
            vm((2, row_tiles, vec, TILE), f32),
            vm((2, col_tiles, vec, TILE), f32),
            vm((2, n_col, share, vec, TILE), f32),
            vm((2, n_row, share, vec, TILE), f32),
            vm((2, share, vec, TILE), f32),
            vm((row_tiles, vec, TILE), f32),
            vm((col_tiles, vec, TILE), f32),
            vm((row_tiles, vec, TILE), f32),
            vm((n_row, vec, 128), f32),
            vm((n_col, vec, 128), f32),
            pltpu.SMEM(((row_tiles + col_tiles) * slots,), f32),
            pltpu.SemaphoreType.DMA((copies,)),
            pltpu.SemaphoreType.DMA((copies,)),
            pltpu.SemaphoreType.DMA(((chunks + 1) * share,)),
        ],
        compiler_params=pltpu.CompilerParams(
            collective_id=0, has_side_effects=True, vmem_limit_bytes=52 * 2**20
        ),
    )(pairs.transpose(0, 1, 3, 2), valid, positions.transpose(1, 0, 2), vectors)
    mean = total[:, :1] / (block * n_row)
    return second / jnp.sqrt(mean + 1e-06)


def solution(mesh):
    placed = (
        P(None, None, "row"),
        P(None, "row"),
        P("row", "col", None, None),
        P("row", "col", None),
    )
    body = functools.partial(per_device, mesh.shape["row"], mesh.shape["col"])
    return jax.shard_map(body, mesh=mesh, in_specs=placed, out_specs=P(None, "row"), check_vma=False)
```

```python
import functools

import jax
import jax.numpy as jnp
from jax import lax
from jax.experimental import pallas as pl
from jax.experimental.pallas import tpu as pltpu
from jax.sharding import PartitionSpec as P

TILE = 512
GROUP = 4
HALF = TILE // 2
MESH = pl.DeviceIdType.MESH


def pieces(x):
    high = x.astype(jnp.bfloat16).astype(jnp.float32)
    rest = x - high
    mid = rest.astype(jnp.bfloat16).astype(jnp.float32)
    return high, mid, rest - mid


def stacked(v):
    high = v.astype(jnp.bfloat16).astype(jnp.float32)
    return jnp.concatenate([high, v - high], axis=0).astype(jnp.bfloat16)


def pack(rows):
    return jnp.concatenate([rows[:, :HALF], rows[:, HALF:]], axis=0)


def turn(x):
    return jnp.concatenate([x[GROUP:], x[:GROUP]], axis=0)


def unpack(x):
    return jnp.concatenate([x, turn(x)], axis=1)


def terms(x, left):
    cut = [pieces(v) for v in x]
    x1, x2, x3 = ([v[i] for v in cut] for i in range(3))
    norm = list(pieces(-0.5 * (x[0] * x[0] + x[1] * x[1] + x[2] * x[2])))
    one = [jnp.ones((2 * GROUP, TILE), jnp.float32)] * 3
    if left:
        parts = x1 + x1 + x2 + x1 + x2 + x3 + norm + one
    else:
        parts = x1 + x2 + x1 + x3 + x2 + x1 + one + norm
    first = lax.broadcasted_iota(jnp.int32, (2 * GROUP, TILE), 0) < GROUP
    fill = jnp.zeros((4 * 2 * GROUP, TILE), jnp.float32)
    both = [jnp.where(first, parts[i], turn(parts[i + 1])) for i in range(0, 24, 2)]
    return jnp.concatenate(both + [fill], axis=0)


def kernel(
    n_row, n_col, nz, ny, chunks, pairs_ref, valid_ref, pos_ref, vec_ref, out_ref, tot_ref, *scratch
):
    far_pos = scratch[:chunks]
    (
        far_vec, row_vec, left_ref, partial_k, k_high, k_low, to_row, to_col,
        row_sum, col_sum, row_recv, col_recv, own_buf,
        first_row, first_col, second_row, sq_recv, tot_recv,
        weight_ref, ssem, rsem,
    ) = scratch[chunks:]
    slots = to_row.shape[0]
    row_tiles = pos_ref.shape[2] // TILE
    share = row_tiles // n_col
    col_tiles = share * n_row
    far = list(far_pos) + [far_vec]
    r = lax.axis_index("row")
    c = lax.axis_index("col")
    z, y = r // ny, r % ny

    def tile_at(tile):
        return pl.ds(pl.multiple_of(tile * TILE, TILE), TILE)

    for t in range(share):
        cut = tile_at(c * share + t)
        at = r * share + t
        for q in range(3):
            rows = pos_ref[q, :, cut]
            for chunk in range(chunks):
                far[chunk][at, q] = pack(rows[chunk * GROUP : (chunk + 1) * GROUP])
        far_vec[at] = vec_ref[:, cut]
    for t in range(row_tiles):
        row_vec[t] = vec_ref[:, t * TILE : (t + 1) * TILE]

    barrier = pltpu.get_barrier_semaphore()
    for k in range(1, n_row):
        pl.semaphore_signal(barrier, inc=1, device_id={"row": (r + k) % n_row}, device_id_type=MESH)
    for k in range(1, n_col):
        pl.semaphore_signal(barrier, inc=1, device_id={"col": (c + k) % n_col}, device_id_type=MESH)
    pl.semaphore_wait(barrier, n_row + n_col - 2)

    sends = []
    counter = [0]

    def next_sem():
        counter[0] += 1
        return counter[0] - 1

    def copy(src, dst, at, device):
        return pltpu.make_async_remote_copy(
            src_ref=src, dst_ref=dst, send_sem=ssem.at[at], recv_sem=rsem.at[at],
            device_id=device, device_id_type=MESH,
        )

    def place(row, chunk):
        return far[chunk].at[pl.ds(row * share, share)]

    def own(chunk):
        return place(r, chunk)

    z_sem = [[next_sem() for _ in range(nz)] for _ in range(chunks + 1)]
    y_sem = [[[next_sem() for _ in range(ny)] for _ in range(nz)] for _ in range(chunks + 1)]

    def z_copy(chunk, k):
        return copy(own(chunk), place(r, chunk), z_sem[chunk][k], {"row": (z + k) % nz * ny + y})

    def z_arrival(chunk, k):
        row = (z - k + nz) % nz * ny + y
        return copy(own(chunk), place(row, chunk), z_sem[chunk][k], {"row": (z + k) % nz * ny + y})

    def y_copy(chunk, k, j):
        row = (z - k + nz) % nz * ny + y
        src = own(chunk) if k == 0 else place(row, chunk)
        return copy(src, place(row, chunk), y_sem[chunk][k][j], {"row": z * ny + (y + j) % ny})

    def y_arrival(chunk, k, j):
        row = (z - k + nz) % nz * ny + (y - j + ny) % ny
        return copy(own(chunk), place(row, chunk), y_sem[chunk][k][j], {"row": z * ny + (y + j) % ny})

    def start_z(chunk):
        for k in reversed(range(1, nz)):
            z_copy(chunk, k).start()
        for j in range(1, ny):
            y_copy(chunk, 0, j).start()

    def forward(chunk, k):
        z_arrival(chunk, k).wait_recv()
        for j in range(1, ny):
            y_copy(chunk, k, j).start()

    def await_y(chunk):
        for k in range(nz):
            for j in range(1, ny):
                y_arrival(chunk, k, j).wait_recv()

    start_z(0)
    def prepare(tile, carry):
        rows = [pos_ref[q, :, tile_at(tile)] for q in range(3)]
        for chunk in range(chunks):
            at = chunk * GROUP // 8 * 8
            own_rows = [v[at : at + 8] for v in rows]
            if chunk * GROUP % 8:
                own_rows = [turn(v) for v in own_rows]
            left_ref[tile, chunk] = jnp.transpose(terms(own_rows, True)).astype(jnp.bfloat16)
        for k in range(1, nz):

            @pl.when(tile == k * row_tiles // nz)
            def _():
                forward(0, k)

        return carry

    lax.fori_loop(0, row_tiles, prepare, 0)
    for slot in range(slots):
        a, b, live = pairs_ref[0, 0, 0, slot], pairs_ref[0, 0, 1, slot], valid_ref[0, 0, slot]
        cross = r * row_tiles + a != b // share * row_tiles + c * share + b % share
        both = jnp.where(cross, live, 0)
        for t in range(row_tiles):
            weight_ref[t * slots + slot] = jnp.where(a == t, live, 0).astype(jnp.float32)
        for t in range(col_tiles):
            weight_ref[(row_tiles + t) * slots + slot] = jnp.where(b == t, both, 0).astype(jnp.float32)
    start_z(1)
    await_y(0)

    def apply_slot(slot, near_row, near_col):
        high, low = k_high[slot], k_low[slot]
        vr, vc = stacked(near_row), stacked(near_col)
        nt = (((1,), (1,)), ((), ()))
        nn = (((1,), (0,)), ((), ()))
        dot = functools.partial(lax.dot_general, preferred_element_type=jnp.float32)
        rows = dot(vc, high, nt) + dot(vc, low, nt)
        cols = dot(vr, high, nn) + dot(vr, low, nn)
        to_row[slot] = rows[:8] + rows[8:]
        to_col[slot] = cols[:8] + cols[8:]

    def apply_first(slot):
        a, b = pairs_ref[0, 0, 0, slot], pairs_ref[0, 0, 1, slot]
        apply_slot(slot, row_vec[a], far_vec[b])

    def form(slot, chunk):
        a, b = pairs_ref[0, 0, 0, slot], pairs_ref[0, 0, 1, slot]
        block = far_pos[chunk][b]
        right = terms([unpack(block[q]) for q in range(3)], False).astype(jnp.bfloat16)
        right = right.reshape(8, 16, TILE)
        spot = lax.broadcasted_iota(jnp.int32, (16, TILE), 0) % GROUP
        masked = []
        for s in range(GROUP):
            keep = jnp.where(spot == s, 1.0, 0.0).astype(jnp.bfloat16)
            masked.append((right * keep[None]).reshape(128, TILE))
        left = left_ref[a, chunk]
        for at in range(0, TILE, 128):
            cut = slice(at, at + 128)
            total = None
            for pair in range(2):
                two = jnp.concatenate([masked[2 * pair][:, cut], masked[2 * pair + 1][:, cut]], axis=1)
                term = jnp.exp(jnp.dot(left, two, preferred_element_type=jnp.float32))
                term = term[:, :128] + term[:, 128:]
                total = term if total is None else total + term
            if chunk > 0:
                total = total + partial_k[slot, :, cut]
            if chunk < chunks - 1:
                partial_k[slot, :, cut] = total
            else:
                high = total.astype(jnp.bfloat16)
                k_high[slot, :, cut] = high
                k_low[slot, :, cut] = (total - high.astype(jnp.float32)).astype(jnp.bfloat16)

    step = 2 if slots % 2 == 0 else 1
    steps = slots // step
    for chunk in range(chunks):
        last = chunk == chunks - 1

        def body(i, carry, chunk=chunk, last=last):
            if last:
                for j in range(step):
                    apply_first((i - 1) * step + j)
            for j in range(step):
                form(i * step + j, chunk)
            if not last:
                for k in range(1, nz):

                    @pl.when(i == min(steps - 1, k * steps // nz))
                    def _():
                        forward(chunk + 1, k)
                        if chunk + 2 == chunks:
                            forward(chunk + 2, k)
                        if k == nz - 1 and chunk + 2 < chunks:
                            start_z(chunk + 2)
                            if chunk + 3 == chunks:
                                start_z(chunk + 3)

            return carry

        if last:
            for j in range(step):
                form(j, chunk)
            lax.fori_loop(1, steps, body, 0)
            for j in range(step):
                apply_first(slots - step + j)
        else:
            lax.fori_loop(0, steps, body, 0)
            await_y(chunk + 1)
            if chunk + 2 == chunks:
                await_y(chunk + 2)

    def exchange(p):
        arrivals = []
        for t in range(col_tiles):
            acc = jnp.zeros((8, TILE), jnp.float32)
            for slot in range(slots):
                acc = acc + weight_ref[(row_tiles + t) * slots + slot] * to_col[slot]
            col_sum[p, t] = acc
        for k in range(1, n_row):
            to = (r + k) % n_row
            one = copy(
                col_sum.at[p, pl.ds(to * share, share)], col_recv.at[p, k], next_sem(), {"row": to}
            )
            one.start()
            arrivals.append(one)
        for t in range(row_tiles):
            acc = jnp.zeros((8, TILE), jnp.float32)
            for slot in range(slots):
                acc = acc + weight_ref[t * slots + slot] * to_row[slot]
            row_sum[p, t] = acc
        for k in range(1, n_col):
            to = (c + k) % n_col
            one = copy(
                row_sum.at[p, pl.ds(to * share, share)], row_recv.at[p, k], next_sem(), {"col": to}
            )
            one.start()
            arrivals.append(one)
        sends.extend(arrivals)
        total = row_sum[p, pl.ds(c * share, share)] + col_sum[p, pl.ds(r * share, share)]
        for one in arrivals:
            one.wait_recv()
        for k in range(1, n_col):
            total = total + row_recv[p, k]
        for k in range(1, n_row):
            total = total + col_recv[p, k]
        own_buf[p] = total
        return total

    def spread(src, dst_of, axis):
        size, me = (n_row, r) if axis == "row" else (n_col, c)
        arrivals = []
        for k in range(1, size):
            at = next_sem()
            one = copy(src, dst_of(me), at, {axis: (me + k) % size})
            one.start()
            sends.append(one)
            arrivals.append(copy(src, dst_of((me - k + size) % size), at, {axis: (me + k) % size}))
        return arrivals

    total = exchange(0)
    arrivals = spread(own_buf.at[0], lambda i: first_col.at[pl.ds(i * share, share)], "row")
    arrivals += spread(own_buf.at[0], lambda i: first_row.at[pl.ds(i * share, share)], "col")
    first_col[pl.ds(r * share, share)] = total
    first_row[pl.ds(c * share, share)] = total
    for one in arrivals:
        one.wait_recv()

    for slot in range(slots):
        a, b = pairs_ref[0, 0, 0, slot], pairs_ref[0, 0, 1, slot]
        apply_slot(slot, first_row[a], first_col[b])

    total = exchange(1)
    squares = jnp.sum(jnp.sum(total * total, axis=0), axis=1, keepdims=True)
    sq_recv[r] = jnp.broadcast_to(squares, (8, 128))
    square_arrivals = spread(sq_recv.at[r], lambda i: sq_recv.at[i], "row")
    arrivals = spread(own_buf.at[1], lambda i: second_row.at[pl.ds(i * share, share)], "col")
    second_row[pl.ds(c * share, share)] = total
    for one in square_arrivals:
        one.wait_recv()
    tot_recv[c] = jnp.sum(sq_recv[...], axis=0)
    total_arrivals = spread(tot_recv.at[c], lambda i: tot_recv.at[i], "col")
    for one in arrivals:
        one.wait_recv()
    for t in range(row_tiles):
        out_ref[:, t * TILE : (t + 1) * TILE] = second_row[t]
    for one in total_arrivals:
        one.wait_recv()
    tot_ref[...] = jnp.sum(tot_recv[...], axis=0)

    for chunk in range(chunks + 1):
        for k in range(1, nz):
            z_copy(chunk, k).wait_send()
        for k in range(nz):
            for j in range(1, ny):
                y_copy(chunk, k, j).wait_send()
    for one in sends:
        one.wait_send()


def per_device(n_row, n_col, positions, vectors, pairs, valid):
    snaps, _, block = positions.shape
    row_tiles = block // TILE
    share = row_tiles // n_col
    col_tiles = share * n_row
    slots = pairs.shape[2]
    vec = vectors.shape[0]
    ny = 1
    while ny * ny * 4 <= n_row:
        ny *= 2
    nz = n_row // ny
    chunks = snaps // GROUP
    copies = (chunks + 1) * (nz + nz * ny) + 3 * (n_row + n_col) + n_row + 2 * n_col
    f32 = jnp.float32
    vm = pltpu.VMEM
    second, total = pl.pallas_call(
        functools.partial(kernel, n_row, n_col, nz, ny, chunks),
        out_shape=(
            jax.ShapeDtypeStruct((vec, block), f32),
            jax.ShapeDtypeStruct((vec, 128), f32),
        ),
        in_specs=[
            pl.BlockSpec(memory_space=pltpu.SMEM),
            pl.BlockSpec(memory_space=pltpu.SMEM),
            pl.BlockSpec(memory_space=pltpu.VMEM),
            pl.BlockSpec(memory_space=pltpu.VMEM),
        ],
        out_specs=[pl.BlockSpec(memory_space=pltpu.VMEM)] * 2,
        scratch_shapes=[
            *[vm((col_tiles, 3, 2 * GROUP, HALF), f32) for _ in range(chunks)],
            vm((col_tiles, vec, TILE), f32),
            vm((row_tiles, vec, TILE), f32),
            vm((row_tiles, chunks, TILE, 128), jnp.bfloat16),
            vm((slots, TILE, TILE), f32),
            vm((slots, TILE, TILE), jnp.bfloat16),
            vm((slots, TILE, TILE), jnp.bfloat16),
            vm((slots, vec, TILE), f32),
            vm((slots, vec, TILE), f32),
            vm((2, row_tiles, vec, TILE), f32),
            vm((2, col_tiles, vec, TILE), f32),
            vm((2, n_col, share, vec, TILE), f32),
            vm((2, n_row, share, vec, TILE), f32),
            vm((2, share, vec, TILE), f32),
            vm((row_tiles, vec, TILE), f32),
            vm((col_tiles, vec, TILE), f32),
            vm((row_tiles, vec, TILE), f32),
            vm((n_row, vec, 128), f32),
            vm((n_col, vec, 128), f32),
            pltpu.SMEM(((row_tiles + col_tiles) * slots,), f32),
            pltpu.SemaphoreType.DMA((copies,)),
            pltpu.SemaphoreType.DMA((copies,)),
        ],
        compiler_params=pltpu.CompilerParams(
            collective_id=0, has_side_effects=True, vmem_limit_bytes=52 * 2**20
        ),
    )(pairs.transpose(0, 1, 3, 2), valid, positions.transpose(1, 0, 2), vectors)
    mean = total[:, :1] / (block * n_row)
    return second / jnp.sqrt(mean + 1e-06)


def solution(mesh):
    placed = (
        P(None, None, "row"),
        P(None, "row"),
        P("row", "col", None, None),
        P("row", "col", None),
    )
    body = functools.partial(per_device, mesh.shape["row"], mesh.shape["col"])
    return jax.shard_map(body, mesh=mesh, in_specs=placed, out_specs=P(None, "row"), check_vma=False)
```

```python
import functools

import jax
import jax.numpy as jnp
from jax import lax
from jax.experimental import pallas as pl
from jax.experimental.pallas import tpu as pltpu
from jax.sharding import PartitionSpec as P

TILE = 512
GROUP = 4
HALF = TILE // 2
ROWS = 64
MESH = pl.DeviceIdType.MESH


def pieces(x):
    high = x.astype(jnp.bfloat16).astype(jnp.float32)
    rest = x - high
    mid = rest.astype(jnp.bfloat16).astype(jnp.float32)
    return high, mid, rest - mid


def stacked(v):
    high = v.astype(jnp.bfloat16).astype(jnp.float32)
    return jnp.concatenate([high, v - high], axis=0).astype(jnp.bfloat16)


def pack(rows):
    return jnp.concatenate([rows[:, :HALF], rows[:, HALF:]], axis=0)


def turn(x):
    return jnp.concatenate([x[GROUP:], x[:GROUP]], axis=0)


def unpack(x):
    return jnp.concatenate([x, turn(x)], axis=1)


def terms(x, left):
    cut = [pieces(v) for v in x]
    x1, x2, x3 = ([v[i] for v in cut] for i in range(3))
    norm = list(pieces(-0.5 * (x[0] * x[0] + x[1] * x[1] + x[2] * x[2])))
    one = [jnp.ones((2 * GROUP, TILE), jnp.float32)] * 3
    if left:
        parts = x1 + x1 + x2 + x1 + x2 + x3 + norm + one
    else:
        parts = x1 + x2 + x1 + x3 + x2 + x1 + one + norm
    first = lax.broadcasted_iota(jnp.int32, (2 * GROUP, TILE), 0) < GROUP
    fill = jnp.zeros((4 * 2 * GROUP, TILE), jnp.float32)
    both = [jnp.where(first, parts[i], turn(parts[i + 1])) for i in range(0, 24, 2)]
    return jnp.concatenate(both + [fill], axis=0)


def kernel(
    n_row, n_col, nz, ny, chunks, pairs_ref, valid_ref, pos_ref, vec_ref, out_ref, tot_ref, *scratch
):
    far_pos = scratch[:chunks]
    (
        far_vec, row_vec, left_ref, partial_k, k_high, k_low, to_row, to_col,
        row_sum, col_sum, row_recv, col_recv, own_buf,
        first_row, first_col, second_row, sq_recv, tot_recv,
        weight_ref, ssem, rsem,
    ) = scratch[chunks:]
    slots = to_row.shape[0]
    row_tiles = pos_ref.shape[2] // TILE
    share = row_tiles // n_col
    col_tiles = share * n_row
    far = list(far_pos) + [far_vec]
    r = lax.axis_index("row")
    c = lax.axis_index("col")
    z, y = r // ny, r % ny

    def tile_at(tile):
        return pl.ds(pl.multiple_of(tile * TILE, TILE), TILE)

    for t in range(share):
        cut = tile_at(c * share + t)
        at = r * share + t
        for q in range(3):
            rows = pos_ref[q, :, cut]
            for chunk in range(chunks):
                far[chunk][at, q] = pack(rows[chunk * GROUP : (chunk + 1) * GROUP])
        far_vec[at] = vec_ref[:, cut]
    for t in range(row_tiles):
        row_vec[t] = vec_ref[:, t * TILE : (t + 1) * TILE]

    barrier = pltpu.get_barrier_semaphore()
    for k in range(1, n_row):
        pl.semaphore_signal(barrier, inc=1, device_id={"row": (r + k) % n_row}, device_id_type=MESH)
    for k in range(1, n_col):
        pl.semaphore_signal(barrier, inc=1, device_id={"col": (c + k) % n_col}, device_id_type=MESH)
    pl.semaphore_wait(barrier, n_row + n_col - 2)

    sends = []
    counter = [0]

    def next_sem():
        counter[0] += 1
        return counter[0] - 1

    def copy(src, dst, at, device):
        return pltpu.make_async_remote_copy(
            src_ref=src, dst_ref=dst, send_sem=ssem.at[at], recv_sem=rsem.at[at],
            device_id=device, device_id_type=MESH,
        )

    def place(row, chunk):
        return far[chunk].at[pl.ds(row * share, share)]

    def own(chunk):
        return place(r, chunk)

    z_sem = [[next_sem() for _ in range(nz)] for _ in range(chunks + 1)]
    y_sem = [[[next_sem() for _ in range(ny)] for _ in range(nz)] for _ in range(chunks + 1)]

    def z_copy(chunk, k):
        return copy(own(chunk), place(r, chunk), z_sem[chunk][k], {"row": (z + k) % nz * ny + y})

    def z_arrival(chunk, k):
        row = (z - k + nz) % nz * ny + y
        return copy(own(chunk), place(row, chunk), z_sem[chunk][k], {"row": (z + k) % nz * ny + y})

    def y_copy(chunk, k, j):
        row = (z - k + nz) % nz * ny + y
        src = own(chunk) if k == 0 else place(row, chunk)
        return copy(src, place(row, chunk), y_sem[chunk][k][j], {"row": z * ny + (y + j) % ny})

    def y_arrival(chunk, k, j):
        row = (z - k + nz) % nz * ny + (y - j + ny) % ny
        return copy(own(chunk), place(row, chunk), y_sem[chunk][k][j], {"row": z * ny + (y + j) % ny})

    def start_z(chunk):
        for k in reversed(range(1, nz)):
            z_copy(chunk, k).start()
        for j in range(1, ny):
            y_copy(chunk, 0, j).start()

    def forward(chunk, k):
        z_arrival(chunk, k).wait_recv()
        for j in range(1, ny):
            y_copy(chunk, k, j).start()

    def await_y(chunk):
        for k in range(nz):
            for j in range(1, ny):
                y_arrival(chunk, k, j).wait_recv()

    start_z(0)
    def prepare(tile, carry):
        rows = [pos_ref[q, :, tile_at(tile)] for q in range(3)]
        for chunk in range(chunks):
            at = chunk * GROUP // 8 * 8
            own_rows = [v[at : at + 8] for v in rows]
            if chunk * GROUP % 8:
                own_rows = [turn(v) for v in own_rows]
            left_ref[tile, chunk] = jnp.transpose(terms(own_rows, True)).astype(jnp.bfloat16)
        for k in range(1, nz):

            @pl.when(tile == k * row_tiles // nz)
            def _():
                forward(0, k)

        return carry

    lax.fori_loop(0, row_tiles, prepare, 0)
    for slot in range(slots):
        a, b, live = pairs_ref[0, 0, 0, slot], pairs_ref[0, 0, 1, slot], valid_ref[0, 0, slot]
        cross = r * row_tiles + a != b // share * row_tiles + c * share + b % share
        both = jnp.where(cross, live, 0)
        for t in range(row_tiles):
            weight_ref[t * slots + slot] = jnp.where(a == t, live, 0).astype(jnp.float32)
        for t in range(col_tiles):
            weight_ref[(row_tiles + t) * slots + slot] = jnp.where(b == t, both, 0).astype(jnp.float32)
    start_z(1)
    await_y(0)

    def apply_slot(slot, near_row, near_col):
        high, low = k_high[slot], k_low[slot]
        vr, vc = stacked(near_row), stacked(near_col)
        nt = (((1,), (1,)), ((), ()))
        nn = (((1,), (0,)), ((), ()))
        dot = functools.partial(lax.dot_general, preferred_element_type=jnp.float32)
        rows = dot(vc, high, nt) + dot(vc, low, nt)
        cols = dot(vr, high, nn) + dot(vr, low, nn)
        to_row[slot] = rows[:8] + rows[8:]
        to_col[slot] = cols[:8] + cols[8:]

    def apply_first(slot):
        a, b = pairs_ref[0, 0, 0, slot], pairs_ref[0, 0, 1, slot]
        apply_slot(slot, row_vec[a], far_vec[b])

    def put(slot, chunk, rows, cut, total):
        if chunk > 0:
            total = total + partial_k[slot, rows, cut]
        if chunk < chunks - 1:
            partial_k[slot, rows, cut] = total
        else:
            high = total.astype(jnp.bfloat16)
            k_high[slot, rows, cut] = high
            k_low[slot, rows, cut] = (total - high.astype(jnp.float32)).astype(jnp.bfloat16)

    def form(slot, chunk):
        a, b = pairs_ref[0, 0, 0, slot], pairs_ref[0, 0, 1, slot]
        block = far_pos[chunk][b]
        right = terms([unpack(block[q]) for q in range(3)], False).astype(jnp.bfloat16)
        left = left_ref[a, chunk]
        spot = lax.broadcasted_iota(jnp.int32, (ROWS, 128), 1) % GROUP
        keep = [jnp.where(spot == s, 1.0, 0.0).astype(jnp.bfloat16) for s in range(GROUP)]
        streamed = jnp.concatenate(
            [left[at : at + ROWS] * mask for at in range(0, TILE, ROWS) for mask in keep], axis=0
        )
        for at in range(0, TILE, 256):
            cut = slice(at, at + 256)
            exponent = jnp.dot(streamed, right[:, cut], preferred_element_type=jnp.float32)
            for block_at in range(0, TILE, ROWS):
                rows = slice(block_at, block_at + ROWS)
                total = None
                for s in range(GROUP):
                    top = block_at * GROUP + s * ROWS
                    term = jnp.exp(exponent[top : top + ROWS])
                    total = term if total is None else total + term
                put(slot, chunk, rows, cut, total)

    step = 2 if slots % 2 == 0 else 1
    steps = slots // step
    for chunk in range(chunks):
        last = chunk == chunks - 1

        def body(i, carry, chunk=chunk, last=last):
            if last:
                for j in range(step):
                    apply_first((i - 1) * step + j)
            for j in range(step):
                form(i * step + j, chunk)
            if not last:
                for k in range(1, nz):

                    @pl.when(i == min(steps - 1, k * steps // nz))
                    def _():
                        forward(chunk + 1, k)
                        if chunk + 2 == chunks:
                            forward(chunk + 2, k)
                        if k == nz - 1 and chunk + 2 < chunks:
                            start_z(chunk + 2)
                            if chunk + 3 == chunks:
                                start_z(chunk + 3)

            return carry

        if last:
            for j in range(step):
                form(j, chunk)
            lax.fori_loop(1, steps, body, 0)
            for j in range(step):
                apply_first(slots - step + j)
        else:
            lax.fori_loop(0, steps, body, 0)
            await_y(chunk + 1)
            if chunk + 2 == chunks:
                await_y(chunk + 2)

    def exchange(p):
        arrivals = []
        for t in range(col_tiles):
            acc = jnp.zeros((8, TILE), jnp.float32)
            for slot in range(slots):
                acc = acc + weight_ref[(row_tiles + t) * slots + slot] * to_col[slot]
            col_sum[p, t] = acc
        for k in range(1, n_row):
            to = (r + k) % n_row
            one = copy(
                col_sum.at[p, pl.ds(to * share, share)], col_recv.at[p, k], next_sem(), {"row": to}
            )
            one.start()
            arrivals.append(one)
        for t in range(row_tiles):
            acc = jnp.zeros((8, TILE), jnp.float32)
            for slot in range(slots):
                acc = acc + weight_ref[t * slots + slot] * to_row[slot]
            row_sum[p, t] = acc
        for k in range(1, n_col):
            to = (c + k) % n_col
            one = copy(
                row_sum.at[p, pl.ds(to * share, share)], row_recv.at[p, k], next_sem(), {"col": to}
            )
            one.start()
            arrivals.append(one)
        sends.extend(arrivals)
        total = row_sum[p, pl.ds(c * share, share)] + col_sum[p, pl.ds(r * share, share)]
        for one in arrivals:
            one.wait_recv()
        for k in range(1, n_col):
            total = total + row_recv[p, k]
        for k in range(1, n_row):
            total = total + col_recv[p, k]
        own_buf[p] = total
        return total

    def spread(src, dst_of, axis):
        size, me = (n_row, r) if axis == "row" else (n_col, c)
        arrivals = []
        for k in range(1, size):
            at = next_sem()
            one = copy(src, dst_of(me), at, {axis: (me + k) % size})
            one.start()
            sends.append(one)
            arrivals.append(copy(src, dst_of((me - k + size) % size), at, {axis: (me + k) % size}))
        return arrivals

    total = exchange(0)
    arrivals = spread(own_buf.at[0], lambda i: first_col.at[pl.ds(i * share, share)], "row")
    arrivals += spread(own_buf.at[0], lambda i: first_row.at[pl.ds(i * share, share)], "col")
    first_col[pl.ds(r * share, share)] = total
    first_row[pl.ds(c * share, share)] = total
    for one in arrivals:
        one.wait_recv()

    for slot in range(slots):
        a, b = pairs_ref[0, 0, 0, slot], pairs_ref[0, 0, 1, slot]
        apply_slot(slot, first_row[a], first_col[b])

    total = exchange(1)
    squares = jnp.sum(jnp.sum(total * total, axis=0), axis=1, keepdims=True)
    sq_recv[r] = jnp.broadcast_to(squares, (8, 128))
    square_arrivals = spread(sq_recv.at[r], lambda i: sq_recv.at[i], "row")
    arrivals = spread(own_buf.at[1], lambda i: second_row.at[pl.ds(i * share, share)], "col")
    second_row[pl.ds(c * share, share)] = total
    for one in square_arrivals:
        one.wait_recv()
    tot_recv[c] = jnp.sum(sq_recv[...], axis=0)
    total_arrivals = spread(tot_recv.at[c], lambda i: tot_recv.at[i], "col")
    for one in arrivals:
        one.wait_recv()
    for t in range(row_tiles):
        out_ref[:, t * TILE : (t + 1) * TILE] = second_row[t]
    for one in total_arrivals:
        one.wait_recv()
    tot_ref[...] = jnp.sum(tot_recv[...], axis=0)

    for chunk in range(chunks + 1):
        for k in range(1, nz):
            z_copy(chunk, k).wait_send()
        for k in range(nz):
            for j in range(1, ny):
                y_copy(chunk, k, j).wait_send()
    for one in sends:
        one.wait_send()


def per_device(n_row, n_col, positions, vectors, pairs, valid):
    snaps, _, block = positions.shape
    row_tiles = block // TILE
    share = row_tiles // n_col
    col_tiles = share * n_row
    slots = pairs.shape[2]
    vec = vectors.shape[0]
    ny = 1
    while ny * ny * 4 <= n_row:
        ny *= 2
    nz = n_row // ny
    chunks = snaps // GROUP
    copies = (chunks + 1) * (nz + nz * ny) + 3 * (n_row + n_col) + n_row + 2 * n_col
    f32 = jnp.float32
    vm = pltpu.VMEM
    second, total = pl.pallas_call(
        functools.partial(kernel, n_row, n_col, nz, ny, chunks),
        out_shape=(
            jax.ShapeDtypeStruct((vec, block), f32),
            jax.ShapeDtypeStruct((vec, 128), f32),
        ),
        in_specs=[
            pl.BlockSpec(memory_space=pltpu.SMEM),
            pl.BlockSpec(memory_space=pltpu.SMEM),
            pl.BlockSpec(memory_space=pltpu.VMEM),
            pl.BlockSpec(memory_space=pltpu.VMEM),
        ],
        out_specs=[pl.BlockSpec(memory_space=pltpu.VMEM)] * 2,
        scratch_shapes=[
            *[vm((col_tiles, 3, 2 * GROUP, HALF), f32) for _ in range(chunks)],
            vm((col_tiles, vec, TILE), f32),
            vm((row_tiles, vec, TILE), f32),
            vm((row_tiles, chunks, TILE, 128), jnp.bfloat16),
            vm((slots, TILE, TILE), f32),
            vm((slots, TILE, TILE), jnp.bfloat16),
            vm((slots, TILE, TILE), jnp.bfloat16),
            vm((slots, vec, TILE), f32),
            vm((slots, vec, TILE), f32),
            vm((2, row_tiles, vec, TILE), f32),
            vm((2, col_tiles, vec, TILE), f32),
            vm((2, n_col, share, vec, TILE), f32),
            vm((2, n_row, share, vec, TILE), f32),
            vm((2, share, vec, TILE), f32),
            vm((row_tiles, vec, TILE), f32),
            vm((col_tiles, vec, TILE), f32),
            vm((row_tiles, vec, TILE), f32),
            vm((n_row, vec, 128), f32),
            vm((n_col, vec, 128), f32),
            pltpu.SMEM(((row_tiles + col_tiles) * slots,), f32),
            pltpu.SemaphoreType.DMA((copies,)),
            pltpu.SemaphoreType.DMA((copies,)),
        ],
        compiler_params=pltpu.CompilerParams(
            collective_id=0, has_side_effects=True, vmem_limit_bytes=52 * 2**20
        ),
    )(pairs.transpose(0, 1, 3, 2), valid, positions.transpose(1, 0, 2), vectors)
    mean = total[:, :1] / (block * n_row)
    return second / jnp.sqrt(mean + 1e-06)


def solution(mesh):
    placed = (
        P(None, None, "row"),
        P(None, "row"),
        P("row", "col", None, None),
        P("row", "col", None),
    )
    body = functools.partial(per_device, mesh.shape["row"], mesh.shape["col"])
    return jax.shard_map(body, mesh=mesh, in_specs=placed, out_specs=P(None, "row"), check_vma=False)
```

```python
import functools

import jax
import jax.numpy as jnp
from jax import lax
from jax.experimental import pallas as pl
from jax.experimental.pallas import tpu as pltpu
from jax.sharding import PartitionSpec as P

TILE = 512
GROUP = 4
HALF = TILE // 2
MESH = pl.DeviceIdType.MESH


def pieces(x):
    high = x.astype(jnp.bfloat16).astype(jnp.float32)
    rest = x - high
    mid = rest.astype(jnp.bfloat16).astype(jnp.float32)
    return high, mid, rest - mid


def stacked(v):
    high = v.astype(jnp.bfloat16).astype(jnp.float32)
    return jnp.concatenate([high, v - high], axis=0).astype(jnp.bfloat16)


def pack(rows):
    return jnp.concatenate([rows[:, :HALF], rows[:, HALF:]], axis=0)


def turn(x):
    return jnp.concatenate([x[GROUP:], x[:GROUP]], axis=0)


def unpack(x):
    return jnp.concatenate([x, turn(x)], axis=1)


def terms(x, left):
    cut = [pieces(v) for v in x]
    x1, x2, x3 = ([v[i] for v in cut] for i in range(3))
    norm = list(pieces(-0.5 * (x[0] * x[0] + x[1] * x[1] + x[2] * x[2])))
    one = [jnp.ones((2 * GROUP, TILE), jnp.float32)] * 3
    if left:
        parts = x1 + x1 + x2 + x1 + x2 + x3 + norm + one
    else:
        parts = x1 + x2 + x1 + x3 + x2 + x1 + one + norm
    first = lax.broadcasted_iota(jnp.int32, (2 * GROUP, TILE), 0) < GROUP
    fill = jnp.zeros((4 * 2 * GROUP, TILE), jnp.float32)
    both = [jnp.where(first, parts[i], turn(parts[i + 1])) for i in range(0, 24, 2)]
    return jnp.concatenate(both + [fill], axis=0)


def kernel(
    n_row, n_col, nz, ny, chunks, pairs_ref, valid_ref, pos_in, vec_in, out_ref, tot_ref, *scratch
):
    far_pos = scratch[:chunks]
    lefts = scratch[chunks : 2 * chunks]
    (
        far_vec, row_vec, pos_ref, vec_ref, load_sem, partial_k, k_high, k_low, to_row, to_col,
        row_sum, col_sum, row_recv, col_recv, own_buf,
        first_row, first_col, second_row, sq_recv, tot_recv,
        weight_ref, ssem, rsem,
    ) = scratch[2 * chunks :]
    slots = to_row.shape[0]
    row_tiles = pos_ref.shape[2] // TILE
    share = row_tiles // n_col
    col_tiles = share * n_row
    far = list(far_pos) + [far_vec]
    r = lax.axis_index("row")
    c = lax.axis_index("col")
    z, y = r // ny, r % ny

    def tile_at(tile):
        return pl.ds(pl.multiple_of(tile * TILE, TILE), TILE)

    loads = [
        pltpu.make_async_copy(pos_in, pos_ref, load_sem.at[0]),
        pltpu.make_async_copy(vec_in, vec_ref, load_sem.at[1]),
    ]
    for load in loads:
        load.start()

    barrier = pltpu.get_barrier_semaphore()
    for k in range(1, n_row):
        pl.semaphore_signal(barrier, inc=1, device_id={"row": (r + k) % n_row}, device_id_type=MESH)
    for k in range(1, n_col):
        pl.semaphore_signal(barrier, inc=1, device_id={"col": (c + k) % n_col}, device_id_type=MESH)
    for load in loads:
        load.wait()
    for t in range(share):
        cut = tile_at(c * share + t)
        at = r * share + t
        for q in range(3):
            rows = pos_ref[q, :, cut]
            for chunk in range(chunks):
                far[chunk][at, q] = pack(rows[chunk * GROUP : (chunk + 1) * GROUP])
        far_vec[at] = vec_ref[:, cut]
    for t in range(row_tiles):
        row_vec[t] = vec_ref[:, t * TILE : (t + 1) * TILE]

    pl.semaphore_wait(barrier, n_row + n_col - 2)

    sends = []
    counter = [0]

    def next_sem():
        counter[0] += 1
        return counter[0] - 1

    def copy(src, dst, at, device):
        return pltpu.make_async_remote_copy(
            src_ref=src, dst_ref=dst, send_sem=ssem.at[at], recv_sem=rsem.at[at],
            device_id=device, device_id_type=MESH,
        )

    def place(row, chunk):
        return far[chunk].at[pl.ds(row * share, share)]

    def own(chunk):
        return place(r, chunk)

    z_sem = [[next_sem() for _ in range(nz)] for _ in range(chunks + 1)]
    y_sem = [[[next_sem() for _ in range(ny)] for _ in range(nz)] for _ in range(chunks + 1)]

    def z_copy(chunk, k):
        return copy(own(chunk), place(r, chunk), z_sem[chunk][k], {"row": (z + k) % nz * ny + y})

    def z_arrival(chunk, k):
        row = (z - k + nz) % nz * ny + y
        return copy(own(chunk), place(row, chunk), z_sem[chunk][k], {"row": (z + k) % nz * ny + y})

    def y_copy(chunk, k, j):
        row = (z - k + nz) % nz * ny + y
        src = own(chunk) if k == 0 else place(row, chunk)
        return copy(src, place(row, chunk), y_sem[chunk][k][j], {"row": z * ny + (y + j) % ny})

    def y_arrival(chunk, k, j):
        row = (z - k + nz) % nz * ny + (y - j + ny) % ny
        return copy(own(chunk), place(row, chunk), y_sem[chunk][k][j], {"row": z * ny + (y + j) % ny})

    def start_z(chunk):
        for k in reversed(range(1, nz)):
            z_copy(chunk, k).start()
        for j in range(1, ny):
            y_copy(chunk, 0, j).start()

    def forward(chunk, k):
        z_arrival(chunk, k).wait_recv()
        for j in range(1, ny):
            y_copy(chunk, k, j).start()

    def await_y(chunk):
        for k in range(nz):
            for j in range(1, ny):
                y_arrival(chunk, k, j).wait_recv()

    start_z(0)
    def prepare(tile, chunk):
        at = chunk * GROUP // 8 * 8
        own_rows = [pos_ref[q, at : at + 8, tile_at(tile)] for q in range(3)]
        if chunk * GROUP % 8:
            own_rows = [turn(v) for v in own_rows]
        lefts[chunk][tile] = jnp.transpose(terms(own_rows, True)).astype(jnp.bfloat16)

    for tile in range(row_tiles):
        prepare(tile, 0)
    for k in range(1, nz):
        forward(0, k)
    for slot in range(slots):
        a, b, live = pairs_ref[0, 0, 0, slot], pairs_ref[0, 0, 1, slot], valid_ref[0, 0, slot]
        cross = r * row_tiles + a != b // share * row_tiles + c * share + b % share
        both = jnp.where(cross, live, 0)
        for t in range(row_tiles):
            weight_ref[t * slots + slot] = jnp.where(a == t, live, 0).astype(jnp.float32)
        for t in range(col_tiles):
            weight_ref[(row_tiles + t) * slots + slot] = jnp.where(b == t, both, 0).astype(jnp.float32)
    start_z(1)
    await_y(0)

    def apply_slot(slot, near_row, near_col):
        high, low = k_high[slot], k_low[slot]
        vr, vc = stacked(near_row), stacked(near_col)
        nt = (((1,), (1,)), ((), ()))
        nn = (((1,), (0,)), ((), ()))
        dot = functools.partial(lax.dot_general, preferred_element_type=jnp.float32)
        rows = dot(vc, high, nt) + dot(vc, low, nt)
        cols = dot(vr, high, nn) + dot(vr, low, nn)
        to_row[slot] = rows[:8] + rows[8:]
        to_col[slot] = cols[:8] + cols[8:]

    def apply_first(slot):
        a, b = pairs_ref[0, 0, 0, slot], pairs_ref[0, 0, 1, slot]
        apply_slot(slot, row_vec[a], far_vec[b])

    def form(slot, chunk):
        a, b = pairs_ref[0, 0, 0, slot], pairs_ref[0, 0, 1, slot]
        block = far_pos[chunk][b]
        right = terms([unpack(block[q]) for q in range(3)], False).astype(jnp.bfloat16)
        right = right.reshape(8, 16, TILE)
        spot = lax.broadcasted_iota(jnp.int32, (16, TILE), 0) % GROUP
        masked = []
        for s in range(GROUP):
            keep = jnp.where(spot == s, 1.0, 0.0).astype(jnp.bfloat16)
            masked.append((right * keep[None]).reshape(128, TILE))
        left = lefts[chunk][a]
        for at in range(0, TILE, 128):
            cut = slice(at, at + 128)
            total = None
            for pair in range(2):
                two = jnp.concatenate([masked[2 * pair][:, cut], masked[2 * pair + 1][:, cut]], axis=1)
                term = jnp.exp(jnp.dot(left, two, preferred_element_type=jnp.float32))
                term = term[:, :128] + term[:, 128:]
                total = term if total is None else total + term
            if chunk > 0:
                total = total + partial_k[slot, :, cut]
            if chunk < chunks - 1:
                partial_k[slot, :, cut] = total
            else:
                high = total.astype(jnp.bfloat16)
                k_high[slot, :, cut] = high
                k_low[slot, :, cut] = (total - high.astype(jnp.float32)).astype(jnp.bfloat16)

    step = 2 if slots % 2 == 0 else 1
    steps = slots // step
    for chunk in range(chunks):
        last = chunk == chunks - 1

        def body(i, carry, chunk=chunk, last=last):
            if last:
                for j in range(step):
                    apply_first((i - 1) * step + j)
            for j in range(step):
                form(i * step + j, chunk)
            if not last:
                each = -(-row_tiles // steps)
                for j in range(each):
                    prepare(jnp.minimum(i * each + j, row_tiles - 1), chunk + 1)
                for k in range(1, nz):

                    @pl.when(i == min(steps - 1, k * steps // nz))
                    def _():
                        forward(chunk + 1, k)
                        if chunk + 2 == chunks:
                            forward(chunk + 2, k)
                        if k == nz - 1 and chunk + 2 < chunks:
                            start_z(chunk + 2)
                            if chunk + 3 == chunks:
                                start_z(chunk + 3)

            return carry

        if last:
            for j in range(step):
                form(j, chunk)
            lax.fori_loop(1, steps, body, 0)
            for j in range(step):
                apply_first(slots - step + j)
        else:
            lax.fori_loop(0, steps, body, 0)
            await_y(chunk + 1)
            if chunk + 2 == chunks:
                await_y(chunk + 2)

    def exchange(p):
        arrivals = []
        for t in range(col_tiles):
            acc = jnp.zeros((8, TILE), jnp.float32)
            for slot in range(slots):
                acc = acc + weight_ref[(row_tiles + t) * slots + slot] * to_col[slot]
            col_sum[p, t] = acc
        for k in range(1, n_row):
            to = (r + k) % n_row
            one = copy(
                col_sum.at[p, pl.ds(to * share, share)], col_recv.at[p, k], next_sem(), {"row": to}
            )
            one.start()
            arrivals.append(one)
        for t in range(row_tiles):
            acc = jnp.zeros((8, TILE), jnp.float32)
            for slot in range(slots):
                acc = acc + weight_ref[t * slots + slot] * to_row[slot]
            row_sum[p, t] = acc
        for k in range(1, n_col):
            to = (c + k) % n_col
            one = copy(
                row_sum.at[p, pl.ds(to * share, share)], row_recv.at[p, k], next_sem(), {"col": to}
            )
            one.start()
            arrivals.append(one)
        sends.extend(arrivals)
        total = row_sum[p, pl.ds(c * share, share)] + col_sum[p, pl.ds(r * share, share)]
        for one in arrivals:
            one.wait_recv()
        for k in range(1, n_col):
            total = total + row_recv[p, k]
        for k in range(1, n_row):
            total = total + col_recv[p, k]
        own_buf[p] = total
        return total

    def spread(src, dst_of, axis):
        size, me = (n_row, r) if axis == "row" else (n_col, c)
        arrivals = []
        for k in range(1, size):
            at = next_sem()
            one = copy(src, dst_of(me), at, {axis: (me + k) % size})
            one.start()
            sends.append(one)
            arrivals.append(copy(src, dst_of((me - k + size) % size), at, {axis: (me + k) % size}))
        return arrivals

    total = exchange(0)
    arrivals = spread(own_buf.at[0], lambda i: first_col.at[pl.ds(i * share, share)], "row")
    arrivals += spread(own_buf.at[0], lambda i: first_row.at[pl.ds(i * share, share)], "col")
    first_col[pl.ds(r * share, share)] = total
    first_row[pl.ds(c * share, share)] = total
    for one in arrivals:
        one.wait_recv()

    for slot in range(slots):
        a, b = pairs_ref[0, 0, 0, slot], pairs_ref[0, 0, 1, slot]
        apply_slot(slot, first_row[a], first_col[b])

    total = exchange(1)
    squares = jnp.sum(jnp.sum(total * total, axis=0), axis=1, keepdims=True)
    sq_recv[r] = jnp.broadcast_to(squares, (8, 128))
    square_arrivals = spread(sq_recv.at[r], lambda i: sq_recv.at[i], "row")
    arrivals = spread(own_buf.at[1], lambda i: second_row.at[pl.ds(i * share, share)], "col")
    second_row[pl.ds(c * share, share)] = total
    for one in square_arrivals:
        one.wait_recv()
    tot_recv[c] = jnp.sum(sq_recv[...], axis=0)
    total_arrivals = spread(tot_recv.at[c], lambda i: tot_recv.at[i], "col")
    for one in arrivals:
        one.wait_recv()
    for t in range(row_tiles):
        out_ref[:, t * TILE : (t + 1) * TILE] = second_row[t]
    for one in total_arrivals:
        one.wait_recv()
    tot_ref[...] = jnp.sum(tot_recv[...], axis=0)

    for chunk in range(chunks + 1):
        for k in range(1, nz):
            z_copy(chunk, k).wait_send()
        for k in range(nz):
            for j in range(1, ny):
                y_copy(chunk, k, j).wait_send()
    for one in sends:
        one.wait_send()


def per_device(n_row, n_col, positions, vectors, pairs, valid):
    snaps, _, block = positions.shape
    row_tiles = block // TILE
    share = row_tiles // n_col
    col_tiles = share * n_row
    slots = pairs.shape[2]
    vec = vectors.shape[0]
    ny = 1
    while ny * ny * 4 <= n_row:
        ny *= 2
    nz = n_row // ny
    chunks = snaps // GROUP
    copies = (chunks + 1) * (nz + nz * ny) + 3 * (n_row + n_col) + n_row + 2 * n_col
    f32 = jnp.float32
    vm = pltpu.VMEM
    second, total = pl.pallas_call(
        functools.partial(kernel, n_row, n_col, nz, ny, chunks),
        out_shape=(
            jax.ShapeDtypeStruct((vec, block), f32),
            jax.ShapeDtypeStruct((vec, 128), f32),
        ),
        in_specs=[
            pl.BlockSpec(memory_space=pltpu.SMEM),
            pl.BlockSpec(memory_space=pltpu.SMEM),
            pl.BlockSpec(memory_space=pltpu.HBM),
            pl.BlockSpec(memory_space=pltpu.HBM),
        ],
        out_specs=[pl.BlockSpec(memory_space=pltpu.VMEM)] * 2,
        scratch_shapes=[
            *[vm((col_tiles, 3, 2 * GROUP, HALF), f32) for _ in range(chunks)],
            *[vm((row_tiles, TILE, 128), jnp.bfloat16) for _ in range(chunks)],
            vm((col_tiles, vec, TILE), f32),
            vm((row_tiles, vec, TILE), f32),
            vm((3, snaps, block), f32),
            vm((vec, block), f32),
            pltpu.SemaphoreType.DMA((2,)),
            vm((slots, TILE, TILE), f32),
            vm((slots, TILE, TILE), jnp.bfloat16),
            vm((slots, TILE, TILE), jnp.bfloat16),
            vm((slots, vec, TILE), f32),
            vm((slots, vec, TILE), f32),
            vm((2, row_tiles, vec, TILE), f32),
            vm((2, col_tiles, vec, TILE), f32),
            vm((2, n_col, share, vec, TILE), f32),
            vm((2, n_row, share, vec, TILE), f32),
            vm((2, share, vec, TILE), f32),
            vm((row_tiles, vec, TILE), f32),
            vm((col_tiles, vec, TILE), f32),
            vm((row_tiles, vec, TILE), f32),
            vm((n_row, vec, 128), f32),
            vm((n_col, vec, 128), f32),
            pltpu.SMEM(((row_tiles + col_tiles) * slots,), f32),
            pltpu.SemaphoreType.DMA((copies,)),
            pltpu.SemaphoreType.DMA((copies,)),
        ],
        compiler_params=pltpu.CompilerParams(
            collective_id=0, has_side_effects=True, vmem_limit_bytes=52 * 2**20
        ),
    )(pairs.transpose(0, 1, 3, 2), valid, positions.transpose(1, 0, 2), vectors)
    mean = total[:, :1] / (block * n_row)
    return second / jnp.sqrt(mean + 1e-06)


def solution(mesh):
    placed = (
        P(None, None, "row"),
        P(None, "row"),
        P("row", "col", None, None),
        P("row", "col", None),
    )
    body = functools.partial(per_device, mesh.shape["row"], mesh.shape["col"])
    return jax.shard_map(body, mesh=mesh, in_specs=placed, out_specs=P(None, "row"), check_vma=False)
```
